32 devices in a mesh: expert: 16 (over z, y, core), shard: 2 (over x).
Axes of the slice: x: 2, y: 2, z: 4, core: 2. Of those that a mesh axis runs over, the one named last changes fastest.
Arguments:
- tokens: bfloat16 [4096, 2048], P(('expert', 'shard')), may hold values from -6 to 6
- cotangent: bfloat16 [4096, 2048], P(('expert', 'shard')), may hold values from -6 to 6
- routes: int32 [4096, 6], P(('expert', 'shard')), may hold values from 0 to 15, all different within a row; in each aligned block of 128 rows (0 to 127, 128 to 255, ...) at most 64 rows name the same one
- lengths: int32 [16, 3], P('expert'), may hold values from 1 to 128, 256 in all within a row
- doc_order: int32 [16, 3], P('expert'), may hold values from 0 to 2, each once within a row
- attn_gain: float32 [2048], P('shard'), may hold values from 0.25 to 1.75
- query_proj: float32 [2048, 3072], P('shard'), may hold values from -0.125 to 0.125
- latent_proj: float32 [2048, 576], P('shard'), may hold values from -0.125 to 0.125
- latent_gain: float32 [512], P('shard'), may hold values from 0.25 to 1.75
- expand_proj: float32 [512, 4096], P('shard'), may hold values from -0.25 to 0.25
- output_proj: float32 [2048, 2048], P('shard'), may hold values from -0.5 to 0.5
- ffn_gain: float32 [2048], P('shard'), may hold values from 0.25 to 1.75
- router_proj: float32 [2048, 16], P('shard'), may hold values from -0.0625 to 0.0625
- shared_gate: float32 [2048, 1408], P('shard'), may hold values from -0.125 to 0.125
- shared_up: float32 [2048, 1408], P('shard'), may hold values from -0.125 to 0.125
- shared_down: float32 [1408, 2048], P('shard'), may hold values from -0.3125 to 0.3125
- expert_gate: float32 [16, 2048, 1408], P('expert', 'shard'), may hold values from -0.125 to 0.125
- expert_up: float32 [16, 2048, 1408], P('expert', 'shard'), may hold values from -0.125 to 0.125
- expert_down: float32 [16, 1408, 2048], P('expert', 'shard'), may hold values from -0.4375 to 0.4375
Outputs:
- layer_out: float32 [4096, 2048], P(('expert', 'shard'))
- grad_tokens: float32 [4096, 2048], P(('expert', 'shard'))
- grad_attn_gain: float32 [2048], P(('expert', 'shard'))
- grad_query_proj: float32 [2048, 3072], P(('expert', 'shard'))
- grad_latent_proj: float32 [2048, 576], P(('expert', 'shard'))
- grad_latent_gain: float32 [512], P(('expert', 'shard'))
- grad_expand_proj: float32 [512, 4096], P(('expert', 'shard'))
- grad_output_proj: float32 [2048, 2048], P(('expert', 'shard'))
- grad_ffn_gain: float32 [2048], P(('expert', 'shard'))
- grad_router_proj: float32 [2048, 16], P(('expert', 'shard'))
- grad_shared_gate: float32 [2048, 1408], P(('expert', 'shard'))
- grad_shared_up: float32 [2048, 1408], P(('expert', 'shard'))
- grad_shared_down: float32 [1408, 2048], P(('expert', 'shard'))
- grad_expert_gate: float32 [16, 2048, 1408], P('expert', 'shard')
- grad_expert_up: float32 [16, 2048, 1408], P('expert', 'shard')
- grad_expert_down: float32 [16, 1408, 2048], P('expert', 'shard')
The draws below stay inside these ranges and needn't reach their ends.
Inputs may be any that keep to these rules, and one draw needn't show every extreme that they name: `routes`: each row names 6 different experts; among the 128 rows of one device no expert is named more than 64 times, and on some device one expert is named exactly 64 times. `lengths`: each row sums to 256, and its largest entry is exactly 128. `doc_order`: each row is a permutation of 0 to 2.
All inputs are finite; a program needn't handle non-finite values.
Results may differ from the reference program's by a relative error of at most 0.018.
The reference program's roundings to bfloat16 on the way count: a program that leaves them out, or rounds other values in their place, can miss the bound.
Values may be sent and summed in bfloat16 or wider, within the bound.
A program may use at most 448 MiB of HBM per device.

```python
import math
from functools import partial
import jax
import jax.numpy as jnp
import numpy as np
from jax import lax

D = 2048
HEADS = 16
NOPE_DIM = 128
ROPE_DIM = 64
LATENT = 512
V_DIM = 128
EXPERT_FF = 1408
TOPK = 6
NSHARED = 1
TOK_DEV = 128
NSEQ = 3
EXPERTS = 16
CAP = 64
GROUP_TOK = 256
SEQ_MOST = 128
GROUPS = 16
TOKENS = 4096
N_EXPERT = 16
N_SHARD = 2


def raised(array, own_key, source, target, parts, factor):
    def block_of(axis_at):
        return (jnp.arange(array.shape[axis_at]) // (array.shape[axis_at] // parts)).reshape((-1,) + (1,) * (array.ndim - 1 - axis_at))

    one_side = jax.random.permutation(own_key, parts)[block_of(target)]
    second = (block_of(target) + parts // 2) % parts
    return jnp.where((block_of(source) == one_side) | (block_of(source) == second), factor * array, array)


def levels(rng, dims, cuts, low, high):
    loudness, own = 1.0, jax.random.fold_in(rng, 6)
    for dim, parts in cuts:
        steps = jnp.exp(jax.random.uniform(jax.random.fold_in(own, dim), (parts,), jnp.float32, low / len(cuts), high / len(cuts)))
        loudness = loudness * jnp.repeat(steps, dims[dim] // parts).reshape([-1 if axis == dim else 1 for axis in range(len(dims))])
    return loudness


def split_up(count, total, most, skew):
    loads = [(1 << 20) // math.isqrt(grade ** skew) + 1 for grade in range(2, count + 1)]
    rest, counts = total - most - (count - 1), [1] * (count - 1)
    while rest > 0:
        movable = [i for i in range(count - 1) if counts[i] < most]
        pool, left = sum([loads[i] for i in movable]), rest
        for i in movable:
            more = min(most - counts[i], max(1, left * loads[i] // pool), rest)
            counts[i] = counts[i] + more
            rest = rest - more
    return np.array([most] + counts)


def uneven(own_key, number_of, total, most, slope):
    if number_of == 2:
        one = jax.random.randint(own_key, (), max(1, total - most), min(most, total - 1) + 1)
        return jnp.stack([one, total - one])
    sizes = jnp.asarray(split_up(number_of, total, most, slope), jnp.int32)
    couples = (number_of - 1) // 2
    donor, taker = sizes[1:1 + 2 * couples:2], sizes[2:2 + 2 * couples:2]
    margin = jnp.minimum(donor - 1, most - taker)
    shifted = jax.random.randint(jax.random.fold_in(own_key, 1), (couples,), 0, 1 << 20) % (margin + 1)
    sizes = sizes.at[1:1 + 2 * couples:2].set(donor - shifted).at[2:2 + 2 * couples:2].set(taker + shifted)
    return sizes[jax.random.permutation(jax.random.fold_in(own_key, 2), number_of)]


def routed_block(own_key, own, number, rows, count, top, bound, slope):
    sequence = jax.random.permutation(own_key, count)
    packed, common = portions_of(count, rows * top, bound, slope, True), portions_of(count, rows * top, bound, slope, False)
    places = jnp.arange(count)

    def named(tallies, turn):
        used = int((tallies > 0).sum())
        fixed = max(1, used // 4)
        passed = fixed + (places - fixed + turn * (used - fixed)) % max(1, count - fixed)
        return jnp.zeros((count,), jnp.int32).at[sequence[jnp.where(places < fixed, places, passed)]].set(jnp.asarray(tallies, jnp.int32))

    tallies = jnp.where(number % 4 == 0, named(packed, number // 4), named(common, number - number // 4 - 1))
    mixed = jax.random.permutation(jax.random.fold_in(own, 3), count)
    source_of, taker = mixed[0:count // 2 * 2:2], mixed[1:count // 2 * 2:2]
    margin = jnp.minimum(tallies[source_of] - 1, bound - tallies[taker]) // 2
    margin = jnp.where((source_of == sequence[0]) | (taker == sequence[0]) | (tallies[taker] == 0), 0, jnp.maximum(margin, 0))
    passed = jax.random.randint(jax.random.fold_in(own, 4), (count // 2,), 0, 1 << 20) % (margin + 1)
    tallies = tallies.at[source_of].add(-passed).at[taker].add(passed)
    members = jnp.searchsorted(jnp.cumsum(tallies), jnp.arange(rows * top), side="right").astype(jnp.int32)
    listing = members.reshape(top, rows).T
    listing = listing[jax.random.permutation(jax.random.fold_in(own, 1), rows)]
    turn = jax.random.randint(jax.random.fold_in(own, 2), (rows, 1), 0, top)
    return jnp.take_along_axis(listing, (jnp.arange(top)[None, :] + turn) % top, axis=1)


def portions_of(number_of, total, bound, slope, full):
    loads = [(1 << 20) // math.isqrt(grade ** slope) + 1 for grade in range(1, number_of + 1)]
    largest = bound if full else min(bound, max(-(-total // number_of), total * loads[0] // sum(loads)))
    least = 1 if total - largest >= number_of - 1 else 0
    counts, rest = [largest] + [least] * (number_of - 1), total - largest - least * (number_of - 1)
    while rest > 0:
        free = [i for i in range(1, number_of) if counts[i] < largest] or [i for i in range(1, number_of) if counts[i] < bound]
        mass, remaining = sum([loads[i] for i in free]), rest
        for i in free:
            addition = min(bound - counts[i], max(1, remaining * loads[i] // mass), rest)
            counts[i] = counts[i] + addition
            rest = rest - addition
    return np.array(counts)


def bell_draw(rng, extent, scale, limit, shards=(), kind=jnp.bfloat16):
    entries = jax.random.normal(rng, extent, jnp.float32) * scale
    if len(shards) > 0:
        entries = levels(rng, extent, shards, -0.22, 0.18) * entries
    return jnp.clip(entries, min=-limit, max=limit).astype(kind)


def bell_draw_with(rng, extent, scale, most, split, heavy, kind=jnp.bfloat16):
    values = scale * jax.random.normal(rng, extent, jnp.float32)
    if split:
        values = values * levels(rng, extent, split, -0.22, 0.18)
    return jnp.clip(raised(values, jax.random.fold_in(rng, 3), *heavy), -most, most).astype(kind)


def setup_inputs(seed: int = 0) -> dict:
    streams_of = jax.random.split(jax.random.key(seed), 20)
    tokens = bell_draw_with(streams_of[0], (TOKENS, D), 1.0, 6.0, ((0, 32),), (0, 1, 32, 2.75))
    cotangent = bell_draw(streams_of[1], (TOKENS, D), 1.0, 6.0, ((0, 32),))
    routes_keys = jax.random.split(jax.random.fold_in(streams_of[2], 1), TOKENS // TOK_DEV)
    routes_turns = jax.random.permutation(jax.random.fold_in(streams_of[2], 3), TOKENS // TOK_DEV)
    routes = jax.vmap(lambda own, number: routed_block(jax.random.fold_in(streams_of[2], 2), own, number, TOK_DEV, EXPERTS, TOPK, CAP, 2))(routes_keys, routes_turns).reshape((TOKENS, TOPK))
    lengths = jax.vmap(lambda own: uneven(own, NSEQ, GROUP_TOK, SEQ_MOST, 1))(jax.random.split(streams_of[3], GROUPS)).reshape((GROUPS, NSEQ)).astype(jnp.int32)
    doc_order = jax.vmap(lambda own: jax.random.permutation(own, NSEQ))(jax.random.split(streams_of[4], GROUPS)).reshape((GROUPS, NSEQ)).astype(jnp.int32)
    attn_gain = jnp.clip(1.0 + 0.15 * jax.random.normal(streams_of[5], (D,), jnp.float32), 0.25, 1.75)
    query_proj = bell_draw(streams_of[6], (D, HEADS * (NOPE_DIM + ROPE_DIM)), D ** -0.5, 0.125, ((0, 2),), jnp.float32)
    latent_proj = bell_draw(streams_of[7], (D, LATENT + ROPE_DIM), D ** -0.5, 0.125, ((0, 2),), jnp.float32)
    latent_gain = jnp.clip(1.0 + 0.15 * jax.random.normal(streams_of[8], (LATENT,), jnp.float32), 0.25, 1.75)
    expand_proj = bell_draw(streams_of[9], (LATENT, HEADS * (NOPE_DIM + V_DIM)), LATENT ** -0.5, 0.25, ((0, 2),), jnp.float32)
    output_proj = bell_draw(streams_of[10], (HEADS * V_DIM, D), (HEADS * V_DIM // 16) ** -0.5, 0.5, ((0, 2),), jnp.float32)
    ffn_gain = jnp.clip(1.0 + 0.15 * jax.random.normal(streams_of[11], (D,), jnp.float32), 0.25, 1.75)
    router_proj = bell_draw(streams_of[12], (D, EXPERTS), (4 * D) ** -0.5, 0.0625, ((0, 2),), jnp.float32)
    shared_gate = bell_draw(streams_of[13], (D, NSHARED * EXPERT_FF), D ** -0.5, 0.125, ((0, 2),), jnp.float32)
    shared_up = bell_draw(streams_of[14], (D, NSHARED * EXPERT_FF), D ** -0.5, 0.125, ((0, 2),), jnp.float32)
    shared_down = bell_draw(streams_of[15], (NSHARED * EXPERT_FF, D), (NSHARED * EXPERT_FF // 4) ** -0.5, 0.3125, ((0, 2),), jnp.float32)
    expert_gate = bell_draw(streams_of[16], (EXPERTS, D, EXPERT_FF), D ** -0.5, 0.125, ((0, 16), (1, 2)), jnp.float32)
    expert_up = bell_draw(streams_of[17], (EXPERTS, D, EXPERT_FF), D ** -0.5, 0.125, ((0, 16), (1, 2)), jnp.float32)
    expert_down = bell_draw(streams_of[18], (EXPERTS, EXPERT_FF, D), (EXPERT_FF // 8) ** -0.5, 0.4375, ((0, 16), (1, 2)), jnp.float32)
    return {"tokens": tokens, "cotangent": cotangent, "routes": routes, "lengths": lengths, "doc_order": doc_order, "attn_gain": attn_gain, "query_proj": query_proj, "latent_proj": latent_proj, "latent_gain": latent_gain, "expand_proj": expand_proj, "output_proj": output_proj, "ffn_gain": ffn_gain, "router_proj": router_proj, "shared_gate": shared_gate, "shared_up": shared_up, "shared_down": shared_down, "expert_gate": expert_gate, "expert_up": expert_up, "expert_down": expert_down}


@jax.custom_vjp
def reduced_precision(v):
    return lax.optimization_barrier(v.astype(jnp.bfloat16)).astype(jnp.float32)

@jax.custom_vjp
def low_back(v):
    return v

def low_keep(v):
    return (reduced_precision(v), None)

def low_pass(kept, grad):
    return (grad,)

def back_keep(v):
    return (v, None)

def back_low(kept, grad):
    return (reduced_precision(grad),)
reduced_precision.defvjp(low_keep, low_pass)
low_back.defvjp(back_keep, back_low)
norm_eps = 1e-06
masked_score = -1e+30
highest = lax.Precision.HIGHEST

def low_both(values):
    return low_back(reduced_precision(values))

def matmul_hi(left, right):
    return jnp.dot(left, right, precision=highest, preferred_element_type=jnp.float32)

def rms_scale(values, gain_vec):
    return values * lax.rsqrt(lax.optimization_barrier(jnp.mean(values * values, axis=-1, keepdims=True)) + norm_eps) * gain_vec

def rotate(values, cosine, sine_vals):
    half_width = values.shape[-1] // 2
    front_part = values[..., :half_width]
    back_part = values[..., half_width:]
    return jnp.concatenate([front_part * cosine - back_part * sine_vals, back_part * cosine + front_part * sine_vals], axis=-1)

def swish_act(values):
    return values / (1.0 + jnp.exp(-values))

def doc_layout(lengths_row, order_row, count):
    seq_slots = jnp.arange(lengths_row.shape[0], dtype=jnp.int32)
    picked = lax.optimization_barrier(jnp.sum(jnp.where(order_row[:, None] == seq_slots[None, :], lengths_row[None, :], 0), axis=1)).astype(jnp.int32)
    seq_ends = jnp.cumsum(picked).astype(jnp.int32)
    seq_starts = (seq_ends - picked).astype(jnp.int32)
    places = jnp.arange(count, dtype=jnp.int32)
    segment = lax.optimization_barrier(jnp.sum((places[:, None] >= seq_ends[None, :]).astype(jnp.int32), axis=1)).astype(jnp.int32)
    seq_begin = lax.optimization_barrier(jnp.sum(jnp.where(segment[:, None] == seq_slots[None, :], seq_starts[None, :], 0), axis=1)).astype(jnp.int32)
    return ((places - seq_begin).astype(jnp.int32), segment)

def rope_tables(position, width):
    half_width = width // 2
    frequency = jnp.exp(-(2.0 * jnp.arange(half_width, dtype=jnp.float32) / width) * math.log(10000.0))
    angles = position.astype(jnp.float32)[:, None] * frequency[None, :]
    return (jnp.cos(angles), jnp.sin(angles))

def reference(tokens, cotangent, routes, lengths, doc_order, attn_gain, query_proj, latent_proj, latent_gain, expand_proj, output_proj, ffn_gain, router_proj, shared_gate, shared_up, shared_down, expert_gate, expert_up, expert_down):
    group_rows = TOK_DEV * N_SHARD
    groups = N_EXPERT
    devices = N_EXPERT * N_SHARD
    score_scale = 1.0 / math.sqrt(NOPE_DIM + ROPE_DIM)
    position, segment = jax.vmap(partial(doc_layout, count=group_rows))(lengths, doc_order)
    cosine, sine_vals = rope_tables(position.reshape(-1), ROPE_DIM)
    cosine = cosine.reshape(groups, group_rows, ROPE_DIM // 2)
    sine_vals = sine_vals.reshape(groups, group_rows, ROPE_DIM // 2)
    places = jnp.arange(group_rows, dtype=jnp.int32)
    causal = places[None, :] <= places[:, None]
    expert_ids = jnp.arange(EXPERTS, dtype=jnp.int32)
    chosen_mask = routes[:, :, None] == expert_ids[None, None, :]
    dev_routes = routes.reshape(devices, TOK_DEV * TOPK)
    onehot = (dev_routes[:, :, None] == expert_ids[None, None, :]).astype(jnp.int32)
    running = jnp.cumsum(onehot, axis=1).astype(jnp.int32)
    slot_index = (lax.optimization_barrier(jnp.sum(onehot * running, axis=2)) - 1).astype(jnp.int32)
    dev_ids = jnp.arange(devices, dtype=jnp.int32)[:, None]
    entry_pos = ((dev_routes * devices + dev_ids) * CAP + slot_index).reshape(-1).astype(jnp.int32)
    token_ids = (jnp.arange(TOKENS * TOPK, dtype=jnp.int32) // TOPK).astype(jnp.int32)
    sequence_slot_lookup = jnp.full((EXPERTS * devices * CAP,), TOKENS, dtype=jnp.int32).at[entry_pos].set(token_ids)
    sequence_slot_lookup = sequence_slot_lookup.reshape(EXPERTS, devices * CAP)

    def forward_pass(input_rows, attention_gain_matrix, query_matrix, latent_matrix, latent_gain_matrix, expand_matrix, output_matrix, feedforward_gain_matrix, router_matrix, shared_gate_matrix, shared_up_matrix, shared_down_matrix, expert_gate_matrix, expert_up_matrix, expert_down_matrix):
        gain_attn_w = reduced_precision(attention_gain_matrix)
        query_w = reduced_precision(query_matrix)
        latent_w = reduced_precision(latent_matrix)
        gain_latent_w = reduced_precision(latent_gain_matrix)
        expand_w = reduced_precision(expand_matrix)
        output_w = reduced_precision(output_matrix)
        gain_ffn_w = reduced_precision(feedforward_gain_matrix)
        router_w = reduced_precision(router_matrix)
        sgate_w = reduced_precision(shared_gate_matrix)
        sup_w = reduced_precision(shared_up_matrix)
        sdown_w = reduced_precision(shared_down_matrix)
        expert_gate_weight = reduced_precision(expert_gate_matrix)
        expert_up_weight = reduced_precision(expert_up_matrix)
        expert_down_weight = reduced_precision(expert_down_matrix)
        normed_one = reduced_precision(rms_scale(input_rows, gain_attn_w))

        def attend(block_in):
            normed, cos_group, sin_group, seg_group = block_in
            query_raw = low_back(matmul_hi(normed, query_w))
            latent_raw = low_back(matmul_hi(normed, latent_w))
            latent_vals = reduced_precision(rms_scale(latent_raw[:, :LATENT], gain_latent_w))
            key_rope = reduced_precision(rotate(latent_raw[:, LATENT:], cos_group, sin_group))
            expanded = low_both(matmul_hi(latent_vals, expand_w)).reshape(group_rows, HEADS, NOPE_DIM + V_DIM)
            keys_all = jnp.concatenate([expanded[:, :, :NOPE_DIM], jnp.broadcast_to(key_rope[:, None, :], (group_rows, HEADS, ROPE_DIM))], axis=-1)
            values_all = expanded[:, :, NOPE_DIM:]
            query_heads = query_raw.reshape(group_rows, HEADS, NOPE_DIM + ROPE_DIM)
            queries = reduced_precision(jnp.concatenate([query_heads[:, :, :NOPE_DIM], rotate(query_heads[:, :, NOPE_DIM:], cos_group[:, None, :], sin_group[:, None, :])], axis=-1))
            scores = low_back(jnp.einsum('qhd,khd->hqk', queries, keys_all, precision=highest)) * score_scale
            visible = (seg_group[:, None] == seg_group[None, :]) & causal
            scores = jnp.where(visible[None], scores, masked_score)
            top_score = lax.optimization_barrier(jnp.max(scores, axis=-1, keepdims=True))
            exp_terms = jnp.exp(scores - top_score)
            attn_probs = exp_terms / lax.optimization_barrier(jnp.sum(exp_terms, axis=-1, keepdims=True))
            attended = low_both(jnp.einsum('hqk,khd->qhd', reduced_precision(attn_probs), values_all, precision=highest))
            return low_back(matmul_hi(attended.reshape(group_rows, HEADS * V_DIM), output_w))
        attn_out = lax.map(jax.checkpoint(attend), (normed_one.reshape(groups, group_rows, D), cosine, sine_vals, segment))
        resid = input_rows + attn_out.reshape(TOKENS, D)
        normed_two = reduced_precision(rms_scale(resid, gain_ffn_w))
        logits = low_back(matmul_hi(normed_two, router_w))
        chosen = lax.optimization_barrier(jnp.sum(jnp.where(chosen_mask, logits[:, None, :], 0.0), axis=-1))
        gate_top = lax.optimization_barrier(jnp.max(chosen, axis=-1, keepdims=True))
        gate_exp = jnp.exp(chosen - gate_top)
        gates = gate_exp / lax.optimization_barrier(jnp.sum(gate_exp, axis=-1, keepdims=True))
        shared_pre = low_back(matmul_hi(normed_two, sgate_w))
        shared_lin = low_back(matmul_hi(normed_two, sup_w))
        shared_act = reduced_precision(swish_act(shared_pre) * shared_lin)
        shared_out = low_back(matmul_hi(shared_act, sdown_w))
        padded = jnp.concatenate([normed_two, jnp.zeros((1, D), dtype=jnp.float32)], axis=0)

        def apply_expert(block_in):
            row_index, gate_mat, up_mat, down_mat = block_in
            row_vals = low_back(padded[row_index])
            pre_gate = low_back(matmul_hi(row_vals, gate_mat))
            lin_part = low_back(matmul_hi(row_vals, up_mat))
            act_vals = reduced_precision(swish_act(pre_gate) * lin_part)
            return low_both(matmul_hi(act_vals, down_mat))
        expert_built = lax.map(jax.checkpoint(apply_expert), (sequence_slot_lookup, expert_gate_weight, expert_up_weight, expert_down_weight))
        picked = expert_built.reshape(-1, D)[entry_pos].reshape(TOKENS, TOPK, D)
        mixture = lax.optimization_barrier(jnp.sum(gates[:, :, None] * picked, axis=1))
        return resid + mixture + shared_out
    layer_out, pullback = jax.vjp(forward_pass, tokens.astype(jnp.float32), attn_gain, query_proj, latent_proj, latent_gain, expand_proj, output_proj, ffn_gain, router_proj, shared_gate, shared_up, shared_down, expert_gate, expert_up, expert_down)
    gradients = pullback(cotangent.astype(jnp.float32))
    return (layer_out, gradients[0], gradients[1], gradients[2], gradients[3], gradients[4], gradients[5], gradients[6], gradients[7], gradients[8], gradients[9], gradients[10], gradients[11], gradients[12], gradients[13], gradients[14])
```

```python
import math

import jax
import jax.numpy as jnp
from jax import lax
from jax.sharding import PartitionSpec as P

HEADS = 16
NOPE_DIM = 128
ROPE_DIM = 64
LATENT = 512
V_DIM = 128
NORM_EPS = 1e-06
MASKED = -1e30
BF = jnp.bfloat16
F32 = jnp.float32
PAIR = [(0, 1), (1, 0)]


def dot(left, right, dims=((1,), (0,))):
    return lax.dot_general(left, right, (dims, ((), ())), preferred_element_type=F32)


def shard_gather(block):
    if lax.axis_size("shard") != 2:
        return lax.all_gather(block, "shard", axis=0, tiled=True)
    other = lax.ppermute(block, "shard", PAIR)
    first = lax.axis_index("shard") == 0
    return jnp.concatenate([jnp.where(first, block, other), jnp.where(first, other, block)], axis=0)


def shard_scatter(partial):
    count = lax.axis_size("shard")
    me = lax.axis_index("shard")
    rows = partial.shape[0] // count
    if count != 2:
        blocks = partial.astype(BF).reshape((count, rows) + partial.shape[1:])
        got = lax.all_to_all(blocks, "shard", split_axis=0, concat_axis=0, tiled=True)
        return jnp.sum(got.astype(F32), axis=0)
    mine = lax.dynamic_slice_in_dim(partial, me * rows, rows, 0)
    theirs = lax.dynamic_slice_in_dim(partial, (1 - me) * rows, rows, 0)
    got = lax.ppermute(theirs.astype(BF), "shard", PAIR)
    return mine.astype(F32) + got.astype(F32)


def shard_sum(partial):
    count = lax.axis_size("shard")
    if count != 2:
        return jnp.sum(lax.all_gather(partial.astype(BF), "shard").astype(F32), axis=0)
    return partial + lax.ppermute(partial.astype(BF), "shard", PAIR).astype(F32)


def shard_transpose(block):
    count = lax.axis_size("shard")
    if count != 2:
        return lax.all_to_all(block, "shard", split_axis=0, concat_axis=1, tiled=True)
    me = lax.axis_index("shard")
    rows = block.shape[0] // 2
    mine = lax.dynamic_slice_in_dim(block, me * rows, rows, 0)
    theirs = lax.dynamic_slice_in_dim(block, (1 - me) * rows, rows, 0)
    got = lax.ppermute(theirs, "shard", PAIR)
    first = me == 0
    return jnp.concatenate([jnp.where(first, mine, got), jnp.where(first, got, mine)], axis=1)


def place_halves(mine, theirs):
    me = lax.axis_index("shard")
    rows = mine.shape[0]
    full = jnp.zeros((2 * rows,) + mine.shape[1:], mine.dtype)
    full = lax.dynamic_update_slice_in_dim(full, mine, me * rows, 0)
    return lax.dynamic_update_slice_in_dim(full, theirs, (1 - me) * rows, 0)


def own_columns(weight, parts, me):
    return jnp.concatenate(
        [
            lax.dynamic_slice_in_dim(weight[i], me * width, width, 1) if width else weight[i]
            for i, width in enumerate(parts)
        ],
        axis=1,
    ).astype(BF)


def column_blocks(weights, parts):
    count = lax.axis_size("shard")
    me = lax.axis_index("shard")
    ranks = lax.axis_size("expert")
    rank = lax.axis_index("expert")
    rows = weights[0].shape[0]
    some = rows // ranks
    strip = [lax.dynamic_slice_in_dim(w, rank * some, some, 0) for w in weights]
    if count != 2:
        packed = jnp.stack([own_columns(strip, parts, s) for s in range(count)])
        crossed = lax.all_to_all(packed, "shard", split_axis=0, concat_axis=0, tiled=True)
        whole = lax.all_gather(crossed, "expert", axis=1, tiled=True)
        return whole.reshape(count * rows, whole.shape[2])
    crossed = lax.ppermute(own_columns(strip, parts, 1 - me), "shard", PAIR)
    theirs = lax.all_gather(crossed, "expert", axis=0, tiled=True)
    return place_halves(own_columns(weights, parts, me), theirs)


def gather_experts(weight):
    low = weight[0].astype(BF)
    if lax.axis_size("shard") != 2:
        return lax.all_gather(low, "shard", axis=0, tiled=True)
    return place_halves(low, lax.ppermute(low, "shard", PAIR))


def rms_scale(values, gain_vec):
    return values * lax.rsqrt(jnp.mean(values * values, axis=-1, keepdims=True) + NORM_EPS) * gain_vec


def rms_back(values, gain_vec, grad):
    inv = lax.rsqrt(jnp.mean(values * values, axis=-1, keepdims=True) + NORM_EPS)
    scaled = grad * gain_vec
    inner = jnp.mean(values * scaled, axis=-1, keepdims=True)
    return inv * scaled - values * (inv * inv * inv * inner), jnp.sum(grad * values * inv, axis=0)


def rotate(values, cosine, sine):
    half = values.shape[-1] // 2
    a, b = values[..., :half], values[..., half:]
    return jnp.concatenate([a * cosine - b * sine, b * cosine + a * sine], axis=-1)


def rotate_back(values, cosine, sine):
    half = values.shape[-1] // 2
    a, b = values[..., :half], values[..., half:]
    return jnp.concatenate([a * cosine + b * sine, b * cosine - a * sine], axis=-1)


def sigmoid(values):
    return 1.0 / (1.0 + jnp.exp(-values))


def doc_layout(lengths_row, order_row, count):
    slots = jnp.arange(lengths_row.shape[0], dtype=jnp.int32)
    picked = jnp.sum(jnp.where(order_row[:, None] == slots[None, :], lengths_row[None, :], 0), axis=1)
    ends = jnp.sum(jnp.where(slots[None, :] <= slots[:, None], picked[None, :], 0), axis=1)
    starts = ends - picked
    places = jnp.arange(count, dtype=jnp.int32)
    segment = jnp.sum((places[:, None] >= ends[None, :]).astype(jnp.int32), axis=1)
    begin = jnp.sum(jnp.where(segment[:, None] == slots[None, :], starts[None, :], 0), axis=1)
    return places - begin, segment


def rope_tables(position, width):
    half = width // 2
    frequency = jnp.exp(-(2.0 * jnp.arange(half, dtype=F32) / width) * math.log(10000.0))
    angles = position.astype(F32)[:, None] * frequency[None, :]
    return jnp.cos(angles), jnp.sin(angles)


def body(
    tokens,
    cotangent,
    routes,
    lengths,
    doc_order,
    attn_gain,
    query_proj,
    latent_proj,
    latent_gain,
    expand_proj,
    output_proj,
    ffn_gain,
    router_proj,
    shared_gate,
    shared_up,
    shared_down,
    expert_gate,
    expert_up,
    expert_down,
):
    shards = lax.axis_size("shard")
    me = lax.axis_index("shard")
    ranks = lax.axis_size("expert")
    rank = lax.axis_index("expert")
    rows, width = tokens.shape
    group = rows * shards
    experts = router_proj.shape[1]
    top = routes.shape[1]
    capacity = min(rows, 4 * rows * top // (3 * experts))
    heads = HEADS // shards
    hidden = shared_gate.shape[1] // shards
    scale = 1.0 / math.sqrt(NOPE_DIM + ROPE_DIM)

    low_tokens = shard_gather(tokens)
    gains = jnp.concatenate([attn_gain, ffn_gain, latent_gain]).astype(BF)[None]
    gains = shard_gather(gains).astype(F32)
    attn_part = attn_gain.shape[0]
    attn_gain_f = gains[:, :attn_part].reshape(-1)
    ffn_gain_f = gains[:, attn_part : 2 * attn_part].reshape(-1)
    latent_gain_f = gains[:, 2 * attn_part :].reshape(-1)
    router_w = shard_gather(router_proj.astype(BF))
    first_w = column_blocks(
        (query_proj, latent_proj), (heads * (NOPE_DIM + ROPE_DIM), 0)
    )
    expand_w = column_blocks((expand_proj,), (heads * (NOPE_DIM + V_DIM),))
    shared_w = column_blocks((shared_gate, shared_up), (hidden, hidden))
    low_cot = shard_gather(cotangent)
    gate_w = gather_experts(expert_gate)
    up_w = gather_experts(expert_up)
    down_w = gather_experts(expert_down)
    output_w = output_proj.astype(BF)
    shared_down_w = shared_down.astype(BF)
    cot_all = lax.all_gather(cotangent, "expert", axis=0, tiled=True)

    position, segment = doc_layout(lengths[0], doc_order[0], group)
    cosine, sine = rope_tables(position, ROPE_DIM)
    place = jnp.arange(group, dtype=jnp.int32)
    visible = (segment[:, None] == segment[None, :]) & (place[None, :] <= place[:, None])
    input_rows = tokens.astype(F32)
    normed_one = rms_scale(low_tokens.astype(F32), attn_gain_f).astype(BF)
    raw = dot(normed_one, first_w)
    query_cols = heads * (NOPE_DIM + ROPE_DIM)
    query_heads = raw[:, :query_cols].reshape(group, heads, NOPE_DIM + ROPE_DIM)
    latent_raw = raw[:, query_cols : query_cols + LATENT]
    latent = rms_scale(latent_raw, latent_gain_f).astype(BF)
    key_rope = rotate(raw[:, query_cols + LATENT :], cosine, sine).astype(BF)
    expanded = dot(latent, expand_w).astype(BF).reshape(group, heads, NOPE_DIM + V_DIM)
    keys = jnp.concatenate(
        [
            expanded[:, :, :NOPE_DIM],
            jnp.broadcast_to(key_rope[:, None, :], (group, heads, ROPE_DIM)),
        ],
        axis=-1,
    )
    values = expanded[:, :, NOPE_DIM:]
    queries = jnp.concatenate(
        [
            query_heads[:, :, :NOPE_DIM],
            rotate(query_heads[:, :, NOPE_DIM:], cosine[:, None, :], sine[:, None, :]),
        ],
        axis=-1,
    ).astype(BF)
    scores = jnp.einsum("qhd,khd->hqk", queries, keys, preferred_element_type=F32) * scale
    scores = jnp.where(visible[None], scores, MASKED)
    top_score = jnp.max(scores, axis=-1, keepdims=True)
    weights = jnp.exp(scores - top_score)
    probs = weights / jnp.sum(weights, axis=-1, keepdims=True)
    probs_low = probs.astype(BF)
    attended = (
        jnp.einsum("hqk,khd->qhd", probs_low, values, preferred_element_type=F32)
        .astype(BF)
        .reshape(group, heads * V_DIM)
    )
    resid = input_rows + shard_scatter(dot(attended, output_w))

    normed_two = rms_scale(resid, ffn_gain_f).astype(BF)
    logits = dot(normed_two, router_w)
    expert_ids = jnp.arange(experts, dtype=jnp.int32)
    chosen_mask = routes[:, :, None] == expert_ids[None, None, :]
    chosen = jnp.sum(jnp.where(chosen_mask, logits[:, None, :], 0.0), axis=-1)
    gate_exp = jnp.exp(chosen - jnp.max(chosen, axis=-1, keepdims=True))
    gates = gate_exp / jnp.sum(gate_exp, axis=-1, keepdims=True)
    gate_table = jnp.sum(jnp.where(chosen_mask, gates[:, :, None], 0.0), axis=1)
    used = jnp.sum(chosen_mask.astype(F32), axis=1)
    gate_high = gate_table.astype(BF)
    gate_rest = gate_table - gate_high.astype(F32)
    gate_mid = gate_rest.astype(BF)
    gate_low = (gate_rest - gate_mid.astype(F32)).astype(BF)
    sent = jnp.concatenate(
        [normed_two, gate_high, gate_mid, gate_low, used.astype(BF)], axis=1
    )
    sent_all = lax.all_gather(sent, "expert", axis=0, tiled=True)

    normed_two_g = shard_gather(normed_two)
    shared_raw = dot(normed_two_g, shared_w)
    shared_pre, shared_lin = shared_raw[:, :hidden], shared_raw[:, hidden:]
    shared_sig = sigmoid(shared_pre)
    shared_act = (shared_pre * shared_sig * shared_lin).astype(BF)
    shared_out = shard_scatter(dot(shared_act, shared_down_w))
    shared_act_grad = dot(low_cot, shared_down_w, ((1,), (1,)))
    shared_grads = jnp.concatenate(
        [
            shared_act_grad * shared_lin * (shared_sig * (1.0 + shared_pre * (1.0 - shared_sig))),
            shared_act_grad * (shared_pre * shared_sig),
        ],
        axis=1,
    ).astype(BF)
    shared_back = shard_scatter(dot(shared_grads, shared_w, ((1,), (1,))))
    grad_shared_pair = dot(normed_two_g, shared_grads, ((0,), (0,))).astype(BF)

    extra = sent_all[:, width:].reshape(ranks, rows, 4, experts)
    extra = lax.dynamic_index_in_dim(extra, rank, 3, keepdims=False).astype(F32)
    gate_seen = extra[:, :, 0] + extra[:, :, 1] + extra[:, :, 2]
    used_seen = extra[:, :, 3]
    earlier = (place[:rows, None] < place[None, :rows]).astype(BF)
    order = dot(used_seen.astype(BF), earlier)
    slot = jnp.where(used_seen > 0.5, order, -1.0)
    pick = slot[:, None, :] == jnp.arange(capacity, dtype=F32)[None, :, None]
    pick_low = pick.astype(BF)
    gate_slot = jnp.sum(jnp.where(pick, gate_seen[:, None, :], 0.0), axis=2)
    normed_all = sent_all[:, :width].reshape(ranks, rows, width)
    taken = (
        jnp.einsum("sct,std->scd", pick_low, normed_all, preferred_element_type=F32)
        .astype(BF)
        .reshape(ranks * capacity, width)
    )
    cot_taken = jnp.einsum(
        "sct,std->scd",
        pick_low,
        cot_all.reshape(ranks, rows, width),
        preferred_element_type=F32,
    )
    mix_grad = (gate_slot[:, :, None] * cot_taken).astype(BF).reshape(ranks * capacity, width)
    pre = dot(taken, gate_w)
    lin = dot(taken, up_w)
    sig = sigmoid(pre)
    act = (pre * sig * lin).astype(BF)
    built = dot(act, down_w).astype(BF).astype(F32).reshape(ranks, capacity, width)
    gate_grad_slot = jnp.sum(cot_taken * built, axis=2)
    gate_grad_seen = jnp.sum(jnp.where(pick, gate_grad_slot[:, :, None], 0.0), axis=1)
    gate_grad_table = lax.all_to_all(
        gate_grad_seen, "expert", split_axis=0, concat_axis=0, tiled=True
    )
    mixed = jnp.einsum(
        "sct,scd->std",
        pick_low,
        (gate_slot[:, :, None] * built).astype(BF),
        preferred_element_type=F32,
    ).astype(BF)
    mixture = lax.psum_scatter(
        mixed.reshape(ranks * rows, width), "expert", scatter_dimension=0, tiled=True
    ).astype(F32)
    act_grad = dot(mix_grad, down_w, ((1,), (1,)))
    pre_grad = (act_grad * lin * (sig * (1.0 + pre * (1.0 - sig)))).astype(BF)
    lin_grad = (act_grad * (pre * sig)).astype(BF)
    rows_grad = (
        dot(pre_grad, gate_w, ((1,), (1,))) + dot(lin_grad, up_w, ((1,), (1,)))
    ).astype(BF)
    rows_back = jnp.einsum(
        "sct,scd->std",
        pick_low,
        rows_grad.reshape(ranks, capacity, width),
        preferred_element_type=F32,
    ).astype(BF)
    normed_grad = lax.psum_scatter(
        rows_back.reshape(ranks * rows, width), "expert", scatter_dimension=0, tiled=True
    ).astype(F32)
    grad_gate_e = shard_scatter(dot(taken, pre_grad, ((0,), (0,))))[None]
    grad_up_e = shard_scatter(dot(taken, lin_grad, ((0,), (0,))))[None]
    grad_down_e = shard_scatter(dot(act, mix_grad, ((0,), (0,))))[None]

    layer_out = resid + mixture + shared_out

    upstream = cotangent.astype(F32)
    gate_grad = gate_grad_table.T
    mean_term = jnp.sum(gate_table * gate_grad, axis=-1, keepdims=True)
    logits_grad = jnp.where(used > 0.5, gate_table * (gate_grad - mean_term), 0.0).astype(BF)
    grad_router = dot(normed_two, logits_grad, ((0,), (0,)))
    normed_grad = normed_grad + dot(logits_grad, router_w, ((1,), (1,))) + shared_back
    resid_part, gain_ffn_grad = rms_back(resid, ffn_gain_f, normed_grad)
    resid_grad = upstream + resid_part
    out_grad = shard_gather(resid_grad.astype(BF))

    half_cols = width // shards
    attended_all = shard_columns(attended)
    own_out_grad = lax.dynamic_slice_in_dim(out_grad, me * half_cols, half_cols, 1)
    grad_output = dot(attended_all, own_out_grad, ((0,), (0,))).astype(BF)
    shared_act_all = shard_columns(shared_act)
    own_cot = lax.dynamic_slice_in_dim(low_cot, me * half_cols, half_cols, 1)
    grad_shared_down = dot(shared_act_all, own_cot, ((0,), (0,))).astype(BF)
    attended_grad = (
        dot(out_grad, output_w, ((1,), (1,))).astype(BF).reshape(group, heads, V_DIM)
    )
    prob_grad = jnp.einsum("qhd,khd->hqk", attended_grad, values, preferred_element_type=F32)
    row_term = jnp.sum(probs * prob_grad, axis=-1, keepdims=True)
    score_grad = (probs * (prob_grad - row_term) * scale).astype(BF)
    query_grad = jnp.einsum("hqk,khd->qhd", score_grad, keys, preferred_element_type=F32)
    key_grad = jnp.einsum("hqk,qhd->khd", score_grad, queries, preferred_element_type=F32)
    value_grad = jnp.einsum(
        "hqk,qhd->khd", probs_low, attended_grad, preferred_element_type=F32
    )
    expanded_grad = (
        jnp.concatenate([key_grad[:, :, :NOPE_DIM], value_grad], axis=-1)
        .astype(BF)
        .reshape(group, heads * (NOPE_DIM + V_DIM))
    )
    rope_grad = jnp.sum(key_grad[:, :, NOPE_DIM:], axis=1)
    grad_expand = dot(latent, expanded_grad, ((0,), (0,))).astype(BF)
    latent_part = dot(expanded_grad, expand_w, ((1,), (1,)))
    latent_sum = shard_sum(jnp.concatenate([latent_part, rope_grad], axis=1))
    latent_rms_grad, _ = rms_back(latent_raw, latent_gain_f, latent_sum[:, :LATENT])
    latent_raw_grad = jnp.concatenate(
        [latent_rms_grad, rotate_back(latent_sum[:, LATENT:], cosine, sine)], axis=-1
    ).astype(BF)
    own_rows = (place // rows == me)[:, None]
    latent_inv = lax.rsqrt(jnp.mean(latent_raw * latent_raw, axis=-1, keepdims=True) + NORM_EPS)
    gain_latent_grad = jnp.sum(
        jnp.where(own_rows, latent_sum[:, :LATENT] * latent_raw * latent_inv, 0.0), axis=0
    )
    query_raw_grad = (
        jnp.concatenate(
            [
                query_grad[:, :, :NOPE_DIM],
                rotate_back(query_grad[:, :, NOPE_DIM:], cosine[:, None, :], sine[:, None, :]),
            ],
            axis=-1,
        )
        .reshape(group, query_cols)
        .astype(BF)
    )
    own_latent = lax.dynamic_slice_in_dim(
        latent_raw_grad, me * (latent_raw_grad.shape[1] // shards), latent_raw_grad.shape[1] // shards, 1
    )
    grad_query = dot(normed_one, query_raw_grad, ((0,), (0,))).astype(BF)
    grad_latent = dot(normed_one, own_latent, ((0,), (0,))).astype(BF)
    raw_grad = jnp.concatenate(
        [query_raw_grad, jnp.where(own_rows, latent_raw_grad, jnp.zeros((), BF))], axis=1
    )
    first_grad = shard_scatter(dot(raw_grad, first_w, ((1,), (1,))))
    input_part, gain_attn_grad = rms_back(input_rows, attn_gain_f, first_grad)
    tokens_grad = resid_grad + input_part

    def spread(grad):
        return lax.psum_scatter(grad, "expert", scatter_dimension=0, tiled=True)

    shared_pair = spread(grad_shared_pair)
    shared_down_part = spread(grad_shared_down)
    output_part = spread(grad_output)
    expand_part = spread(grad_expand)
    latent_cols = spread(grad_latent)
    query_part = spread(grad_query)
    out_query = shard_transpose(query_part).astype(F32)
    out_latent = shard_transpose(latent_cols).astype(F32)
    out_expand = shard_transpose(expand_part).astype(F32)
    out_output = shard_transpose(output_part).astype(F32)
    out_gate = shard_transpose(shared_pair[:, :hidden]).astype(F32)
    out_up = shard_transpose(shared_pair[:, hidden:]).astype(F32)
    out_down = shard_transpose(shared_down_part).astype(F32)

    parts = ranks * shards
    small = jnp.concatenate(
        [
            gain_attn_grad.reshape(parts, -1),
            gain_ffn_grad.reshape(parts, -1),
            gain_latent_grad.reshape(parts, -1),
            grad_router.reshape(parts, -1),
        ],
        axis=1,
    )
    small = lax.psum_scatter(
        small, ("expert", "shard"), scatter_dimension=0, tiled=True
    ).reshape(-1)
    n_attn, n_latent = width // parts, LATENT // parts
    out_attn_gain = small[:n_attn]
    out_ffn_gain = small[n_attn : 2 * n_attn]
    out_latent_gain = small[2 * n_attn : 2 * n_attn + n_latent]
    out_router = small[2 * n_attn + n_latent :].reshape(n_attn, experts)
    return (
        layer_out,
        tokens_grad,
        out_attn_gain,
        out_query,
        out_latent,
        out_latent_gain,
        out_expand,
        out_output,
        out_ffn_gain,
        out_router,
        out_gate,
        out_up,
        out_down,
        grad_gate_e,
        grad_up_e,
        grad_down_e,
    )


def shard_columns(block):
    if lax.axis_size("shard") != 2:
        return lax.all_gather(block, "shard", axis=1, tiled=True)
    other = lax.ppermute(block, "shard", PAIR)
    first = lax.axis_index("shard") == 0
    return jnp.concatenate([jnp.where(first, block, other), jnp.where(first, other, block)], axis=1)


def solution(mesh):
    both = ("expert", "shard")
    rows, cols = P(both, None), P("shard", None)
    owned = P("expert", "shard", None)
    return jax.shard_map(
        body,
        mesh=mesh,
        in_specs=(
            rows,
            rows,
            rows,
            P("expert", None),
            P("expert", None),
            P("shard"),
            cols,
            cols,
            P("shard"),
            cols,
            cols,
            P("shard"),
            cols,
            cols,
            cols,
            cols,
            owned,
            owned,
            owned,
        ),
        out_specs=(
            rows,
            rows,
            P(both),
            rows,
            rows,
            P(both),
            rows,
            rows,
            P(both),
            rows,
            rows,
            rows,
            rows,
            owned,
            owned,
            owned,
        ),
        check_vma=False,
    )
```
